1024 devices in a mesh: blk: 256 (over y, z, core), sub: 4 (over x).
Axes of the slice: x: 4, y: 8, z: 16, core: 2. Of those that a mesh axis runs over, the one named last changes fastest.
Arguments:
- correlation: float32 [2048, 6, 128, 128], P(('blk', 'sub')), may hold values from -3 to 3, as said below
- factor: float32 [2048, 6, 128, 128], P(('blk', 'sub')), may hold values from -2 to 2, as said below
- pattern: int32 [2048, 6], replicated, may hold values from 0 to 2047, as said below
Outputs:
- refined: float32 [2048, 6, 128, 128], P(('blk', 'sub'))
- correction: float32 [2048, 6, 128, 128], P(('blk', 'sub'))
The draws below stay inside these ranges and needn't reach their ends.
Inputs may be any that keep to these rules, and one draw needn't show every extreme that they name: `pattern`: slot 0 of tile row i is i itself; the other 5 slots name all but one of the tile rows i - 3 to i + 3 other than i, taken modulo 2048, in increasing offset. `correlation`: slot 0 of each tile row holds the diagonal tile. `factor`: slot 0 of each tile row holds the diagonal tile.
All inputs are finite; a program needn't handle non-finite values.
Results may differ from the reference program's by a relative error of at most 0.0003.
Values sent between devices are 32-bit elements; how exact they have to be, the bound alone decides.
A program may use at most 64 MiB of HBM per device.

```python
import math
import jax
import jax.numpy as jnp
from jax import lax

TILE = 128
REACH = 3
ITERS = 1
SLOTS = 6
NT = 2048


def draw_pattern(key, part):
    dropped = jax.random.randint(key, (NT, 1), 0, 2 * REACH)
    position = jnp.arange(2 * REACH - 1, dtype=jnp.int32)[None, :]
    chosen = position + (position >= dropped).astype(jnp.int32)
    offset = chosen - REACH + (chosen >= REACH).astype(jnp.int32)
    row_ids = jnp.arange(NT, dtype=jnp.int32)[:, None]
    others = (row_ids + offset) % NT
    return jnp.concatenate([row_ids, others], axis=1).astype(jnp.int32)


def tile_noise(key):
    shape = (NT, SLOTS, TILE, TILE)
    noise = jnp.clip(jax.random.normal(jax.random.fold_in(key, 13), shape), -6.0, 6.0)
    return noise.astype(jnp.float32)


def draw_correlation(key, part):
    scale = 0.6 / math.sqrt(SLOTS * TILE)
    tiles = tile_noise(jax.random.fold_in(key, 1)) * scale
    return tiles.at[:, 0].add(2.0 * jnp.eye(TILE, dtype=jnp.float32))


def draw_factor(key, part):
    scale = 0.4 / math.sqrt(SLOTS * TILE)
    tiles = tile_noise(jax.random.fold_in(key, 2)) * scale
    return tiles.at[:, 0].add(jnp.eye(TILE, dtype=jnp.float32) / math.sqrt(2.0))


def setup_inputs(seed: int = 0) -> dict:
    key_list = jax.random.split(jax.random.key(seed), 4)
    return {
        "correlation": draw_correlation(jax.random.fold_in(key_list[3], 71), 0),
        "factor": draw_factor(jax.random.fold_in(key_list[3], 71), 0),
        "pattern": draw_pattern(jax.random.fold_in(key_list[3], 71), 0),
    }


def lookup(tiles, pattern, rows_wanted, columns_wanted):
    matches = pattern[rows_wanted] == columns_wanted[..., None]
    slot_index = jnp.argmax(matches, axis=-1).astype(jnp.int32)
    present = jnp.any(matches, axis=-1).astype(tiles.dtype)
    return tiles[rows_wanted, slot_index] * present[..., None, None]


def row_product(left_tiles, right_tiles, pattern, row_index):
    own_cols = pattern[row_index]
    width_slots = own_cols.shape[0]
    grid_shape = (width_slots, width_slots)
    chosen = lookup(right_tiles, pattern, jnp.broadcast_to(own_cols[:, None], grid_shape), jnp.broadcast_to(own_cols[None, :], grid_shape))
    return jnp.einsum("qab,qpbc->pac", left_tiles[row_index], chosen, precision=lax.Precision.HIGHEST)


def row_gram(factor, product, pattern, row_index):
    total_rows = pattern.shape[0]
    offsets = jnp.arange(-REACH, REACH + 1, dtype=jnp.int32)
    candidates = (row_index + offsets) % total_rows
    left_side = lookup(factor, pattern, candidates, jnp.broadcast_to(row_index, candidates.shape))
    wanted = pattern[row_index]
    grid_shape = (candidates.shape[0], wanted.shape[0])
    right_side = lookup(product, pattern, jnp.broadcast_to(candidates[:, None], grid_shape), jnp.broadcast_to(wanted[None, :], grid_shape))
    return jnp.einsum("oba,opbc->pac", left_side, right_side, precision=lax.Precision.HIGHEST)


def reference(correlation, factor, pattern):
    total_rows = pattern.shape[0]
    all_rows = jnp.arange(total_rows, dtype=jnp.int32)
    identity = jnp.eye(correlation.shape[2], dtype=jnp.float32)
    correction = factor
    for sweep_index in range(ITERS):
        product = lax.map(lambda row_index: row_product(correlation, factor, pattern, row_index), all_rows)
        gram_tiles = lax.map(lambda row_index: row_gram(factor, product, pattern, row_index), all_rows)
        correction = (-gram_tiles).at[:, 0].add(identity)
        update = lax.map(lambda row_index: row_product(factor, correction, pattern, row_index), all_rows)
        factor = factor + 0.5 * update
    return factor, correction
```

```python
import jax
import jax.numpy as jnp
from jax import lax
from jax.experimental import pallas as pl
from jax.experimental.pallas import tpu as pltpu
from jax.sharding import PartitionSpec as P

T = 128
SLOTS = 6
OFFS = (-3, -2, -1, 1, 2, 3)
F32 = jnp.float32
BF16 = jnp.bfloat16
MESH = pl.DeviceIdType.MESH


def halves(x):
    hi = x.astype(BF16)
    return hi, (x - hi.astype(F32)).astype(BF16)


def dot(a, b):
    return jnp.dot(a, b, preferred_element_type=F32)


def kernel(
    corr_hbm, fact_hbm, pat_hbm, refined_hbm, correction_hbm,
    pat, zraw, sraw, zwin, scat, zh, zl, zth, ztl, psend, pcol, pcat,
    dsend, drow, dcat, usend, urow, dout, uout, lsem, ssem, rsem,
):
    blks, subs = lax.axis_size("blk"), lax.axis_size("sub")
    world = blks * subs
    rows_all = 2 * world
    me = lax.axis_index("blk") * subs + lax.axis_index("sub")

    def device(by):
        d = lax.rem(me + by + world, world)
        return (lax.div(d, subs), lax.rem(d, subs))

    def row_of(w):
        return lax.rem(2 * me + (w - 3) + rows_all, rows_all)

    load_pat = pltpu.make_async_copy(pat_hbm, pat, lsem.at[0])
    load_z = pltpu.make_async_copy(fact_hbm, zraw.at[:, pl.ds(0, SLOTS)], lsem.at[1])
    load_s = pltpu.make_async_copy(corr_hbm, sraw.at[:, pl.ds(0, SLOTS)], lsem.at[2])
    load_z.start()
    load_pat.start()
    load_s.start()

    barrier = pltpu.get_barrier_semaphore()
    for by in (-2, -1, 1, 2):
        pl.semaphore_signal(barrier, inc=1, device_id=device(by), device_id_type=MESH)

    zero = jnp.zeros((T, T), F32)
    for r in range(2):
        zraw[r, SLOTS] = zero
        sraw[r, SLOTS] = zero
    zero16 = jnp.zeros((T, T), BF16)
    for a in range(8):
        for b in range(8):
            if abs(a - b) > 3:
                for ref in (zh, zl, zth, ztl):
                    ref[a * T : (a + 1) * T, b * T : (b + 1) * T] = zero16
    for base in (0, 2 * T):
        scat[base : base + T, 7 * T :] = zero16
        scat[base + T : base + 2 * T, :T] = zero16

    load_pat.wait()
    low = []
    for r in range(2):
        row = row_of(3 + r)
        low.append([None] + [
            (pat[s, row] == row_of(3 + r + OFFS[s - 1])).astype(jnp.int32) for s in range(1, SLOTS)
        ])

    def slot_of(r, p):
        here = jnp.int32(SLOTS) if p == 0 else p + low[r][p] * (SLOTS - p)
        return here if p == 5 else jnp.where(low[r][p + 1] == 1, p + 1, here)

    def present(w, column):
        p = OFFS.index(column - w) if column != w else None
        if p is None:
            return None
        row, want = row_of(w), row_of(column)
        found = jnp.int32(0)
        if p <= 4:
            found = found | (pat[p + 1, row] == want).astype(jnp.int32)
        if p >= 1:
            found = found | (pat[p, row] == want).astype(jnp.int32)
        return found.astype(F32)

    def masked(x, w, column):
        if abs(w - column) > 3:
            return jnp.zeros_like(x)
        m = present(w, column)
        return x if m is None else x * m

    slots = [[slot_of(r, p) for p in range(6)] for r in range(2)]

    def dense(ref, r, o):
        if o == 3:
            return ref[r, 0]
        return ref[r, slots[r][o if o < 3 else o - 1]]

    load_z.wait()
    for r in range(2):
        for o in range(7):
            zwin[3 + r, o] = dense(zraw, r, o)

    pl.semaphore_wait(barrier, 4)

    count = [0]
    started = []

    def send(src, dst, by):
        k = count[0]
        count[0] += 1
        cp = pltpu.make_async_remote_copy(
            src_ref=src, dst_ref=dst, send_sem=ssem.at[k], recv_sem=rsem.at[k],
            device_id=device(by), device_id_type=MESH,
        )
        cp.start()
        started.append(cp)
        return cp

    def send_z(row_from, row_to, o, n, by):
        return send(zwin.at[row_from, pl.ds(o, n)], zwin.at[row_to, pl.ds(o, n)], by)

    r1 = send_z(4, 2, 3, 4, 1)
    l1 = send_z(3, 5, 0, 4, -1)
    r2 = send_z(4, 2, 1, 2, 1)
    l2 = send_z(3, 5, 4, 2, -1)
    r3 = send_z(3, 1, 2, 3, 1)
    l3 = send_z(4, 6, 2, 3, -1)

    def place(w, offsets):
        for o in offsets:
            t = zwin[w, o]
            c = w + o - 3
            hi, lo = halves(t)
            here = (slice(w * T, (w + 1) * T), slice(c * T, (c + 1) * T))
            zh[here] = hi
            zl[here] = lo
            hi, lo = halves(t.T)
            there = here[::-1]
            zth[there] = hi
            ztl[there] = lo

    for r in range(2):
        place(3 + r, range(7))
    load_s.wait()
    for r in range(2):
        for o in range(7):
            hi, lo = halves(dense(sraw, r, o))
            c = r + o
            scat[r * T : (r + 1) * T, c * T : (c + 1) * T] = hi
            scat[(2 + r) * T : (3 + r) * T, c * T : (c + 1) * T] = lo

    r1.wait_recv()
    f1 = send_z(2, 0, 3, 3, 1)
    l1.wait_recv()
    g1 = send_z(5, 7, 1, 3, -1)
    r4 = send_z(3, 1, 5, 2, 1)
    l4 = send_z(4, 6, 0, 2, -1)
    f2 = send_z(2, 0, 6, 1, 1)
    g2 = send_z(5, 7, 0, 1, -1)
    place(2, range(3, 7))
    place(5, range(4))
    r2.wait_recv()
    place(2, range(1, 3))
    l2.wait_recv()
    place(5, range(4, 6))
    r3.wait_recv()
    place(1, range(2, 5))
    l3.wait_recv()
    place(6, range(2, 5))

    def product(rows, columns):
        k, n = slice(rows[0] * T, rows[1] * T), slice(columns[0] * T, columns[1] * T)
        both = dot(scat[:, k], zh[k, n])
        return both[: 2 * T] + both[2 * T :] + dot(scat[: 2 * T, k], zl[k, n])

    def keep_product(x, first, ref, index):
        for n in range(x.shape[1] // T):
            for r in range(2):
                tile = x[r * T : (r + 1) * T, n * T : (n + 1) * T]
                ref[index(first + n, r)] = masked(tile, 3 + r, first + n)

    f1.wait_recv()
    place(0, range(3, 6))
    keep_product(product((0, 6), (0, 3)), 0, psend, lambda c, r: (c, r))
    pl1 = send(psend.at[1], pcol.at[0, pl.ds(5, 2)], -1)
    g1.wait_recv()
    place(7, range(1, 4))
    keep_product(product((2, 8), (5, 8)), 5, psend, lambda c, r: (c, r))
    pr0 = send(psend.at[7, pl.ds(1, 1)], pcol.at[0, pl.ds(0, 1)], 2)
    pr1 = send(psend.at[5], pcol.at[0, pl.ds(1, 2)], 1)
    pl0 = send(psend.at[0, pl.ds(0, 1)], pcol.at[1, pl.ds(7, 1)], -2)
    pr2 = send(psend.at[6], pcol.at[1, pl.ds(1, 2)], 1)
    pl2 = send(psend.at[2], pcol.at[1, pl.ds(5, 2)], -1)

    r4.wait_recv()
    place(1, range(5, 7))
    l4.wait_recv()
    place(6, range(2))
    f2.wait_recv()
    place(0, (6,))
    g2.wait_recv()
    place(7, (0,))
    keep_product(product((0, 8), (3, 5)), 3, pcol, lambda c, r: (c - 3, 3 + r))

    identity = (
        lax.broadcasted_iota(jnp.int32, (T, T), 0) == lax.broadcasted_iota(jnp.int32, (T, T), 1)
    ).astype(F32)

    def banded(high, low_, cat, c):
        here = slice(c * T, (c + 7) * T)
        wide = dot(high[here, here], cat[c])
        return wide[:, :T] + wide[:, T:] + dot(low_[here, here], cat[c, :, :T])

    def gram(c):
        for n in range(7):
            hi, lo = halves(pcol[c, c + n])
            pcat[c, n * T : (n + 1) * T, :T] = hi
            pcat[c, n * T : (n + 1) * T, T:] = lo
        g = banded(zth, ztl, pcat, c)
        for n in range(7):
            w = c + n
            tile = -g[n * T : (n + 1) * T]
            if w == 3 + c:
                tile = tile + identity
            tile = masked(tile, w, 3 + c)
            dsend[c, w] = tile
            if w in (3, 4):
                drow[3 + c, w - 3] = tile
            hi, lo = halves(tile)
            dcat[c, n * T : (n + 1) * T, :T] = hi
            dcat[c, n * T : (n + 1) * T, T:] = lo

    def send_column(src, dst, c):
        if c == 0:
            far = send(src.at[0, pl.ds(0, 1)], dst.at[7, pl.ds(1, 1)], -2)
        else:
            far = send(src.at[1, pl.ds(7, 1)], dst.at[0, pl.ds(0, 1)], 2)
        return [
            far,
            send(src.at[c, pl.ds(5, 2)], dst.at[1 + c], 1),
            send(src.at[c, pl.ds(1, 2)], dst.at[5 + c], -1),
        ]

    def update(c):
        u = banded(zh, zl, dcat, c)
        for n in range(7):
            w = c + n
            tile = u[n * T : (n + 1) * T]
            usend[c, w] = tile
            if w in (3, 4):
                urow[3 + c, w - 3] = tile

    for cp in (pl1, pr0, pr1):
        cp.wait_recv()
    gram(0)
    dcps = send_column(dsend, drow, 0)
    for cp in (pl0, pr2, pl2):
        cp.wait_recv()
    gram(1)
    dcps += send_column(dsend, drow, 1)
    update(0)
    ucps = send_column(usend, urow, 0)
    update(1)
    ucps += send_column(usend, urow, 1)

    def column_of(r, s):
        if s == 0:
            return 3 + r
        position = s - low[r][s]
        return r + position + (position >= 3).astype(jnp.int32)

    for cp in dcps:
        cp.wait_recv()
    for r in range(2):
        for s in range(SLOTS):
            dout[r, s] = drow[column_of(r, s), r]
    keep_d = pltpu.make_async_copy(dout, correction_hbm, lsem.at[3])
    keep_d.start()
    for cp in ucps:
        cp.wait_recv()
    for r in range(2):
        for s in range(SLOTS):
            uout[r, s] = zraw[r, s] + 0.5 * urow[column_of(r, s), r]
    keep_u = pltpu.make_async_copy(uout, refined_hbm, lsem.at[4])
    keep_u.start()
    for cp in started:
        cp.wait_send()
    keep_d.wait()
    keep_u.wait()


COPIES = 12 + 6 + 12


def body(correlation, factor, pattern):
    any_space = pl.BlockSpec(memory_space=pl.ANY)
    out = jax.ShapeDtypeStruct(factor.shape, F32)
    tiles = lambda *lead: pltpu.VMEM((*lead, T, T), F32)
    return pl.pallas_call(
        kernel,
        out_shape=(out, out),
        in_specs=[any_space] * 3,
        out_specs=(any_space, any_space),
        scratch_shapes=[
            pltpu.SMEM(pattern.T.shape, jnp.int32),
            tiles(2, SLOTS + 1),
            tiles(2, SLOTS + 1),
            tiles(8, 7),
            pltpu.VMEM((4 * T, 8 * T), BF16),
            *[pltpu.VMEM((8 * T, 8 * T), BF16)] * 4,
            tiles(8, 2),
            tiles(2, 8),
            pltpu.VMEM((2, 7 * T, 2 * T), BF16),
            tiles(2, 8),
            tiles(8, 2),
            pltpu.VMEM((2, 7 * T, 2 * T), BF16),
            tiles(2, 8),
            tiles(8, 2),
            tiles(2, SLOTS),
            tiles(2, SLOTS),
            pltpu.SemaphoreType.DMA((5,)),
            pltpu.SemaphoreType.DMA((COPIES,)),
            pltpu.SemaphoreType.DMA((COPIES,)),
        ],
        compiler_params=pltpu.CompilerParams(
            collective_id=0, has_side_effects=True, vmem_limit_bytes=48 << 20
        ),
    )(correlation, factor, pattern.T)


def solution(mesh):
    rows = P(("blk", "sub"), None, None, None)
    return jax.shard_map(body, mesh=mesh, in_specs=(rows, rows, P()), out_specs=(rows, rows), check_vma=False)
```

```python
import jax
import jax.numpy as jnp
from jax import lax
from jax.experimental import pallas as pl
from jax.experimental.pallas import tpu as pltpu
from jax.sharding import PartitionSpec as P

T = 128
RING = 32
SLOTS = 6
OFFS = (-3, -2, -1, 1, 2, 3)
F32 = jnp.float32
BF16 = jnp.bfloat16
MESH = pl.DeviceIdType.MESH


def halves(x):
    hi = x.astype(BF16)
    return hi, (x - hi.astype(F32)).astype(BF16)


def dot(a, b):
    return jnp.dot(a, b, preferred_element_type=F32)


def kernel(
    corr_hbm, fact_hbm, pat_hbm, refined, correction,
    pat, zraw, sraw, zwin, scat, zh, zl, zth, ztl, psend, pcol, pcat,
    dsend, drow, dcat, usend, urow, lsem, ssem, rsem, here,
):
    blks, subs = lax.axis_size("blk"), lax.axis_size("sub")
    world = blks * subs
    rows_all = 2 * world
    blk, sub = lax.axis_index("blk"), lax.axis_index("sub")
    me = blk * subs + sub
    opens = (sub == 0) & (lax.rem(blk, RING) == 0)

    def device(by):
        d = lax.rem(me + by + world, world)
        return (lax.div(d, subs), lax.rem(d, subs))

    def row_of(w):
        return lax.rem(2 * me + (w - 3) + rows_all, rows_all)

    load_pat = pltpu.make_async_copy(pat_hbm, pat, lsem.at[0])
    load_z = pltpu.make_async_copy(fact_hbm, zraw.at[:, pl.ds(0, SLOTS)], lsem.at[1])
    load_s = pltpu.make_async_copy(corr_hbm, sraw.at[:, pl.ds(0, SLOTS)], lsem.at[2])
    load_z.start()
    load_pat.start()
    load_s.start()

    barrier = pltpu.get_barrier_semaphore()
    for partner in (device(-1), device(-2)):
        pl.semaphore_signal(barrier, inc=1, device_id=partner, device_id_type=MESH)

    zero = jnp.zeros((T, T), F32)
    for r in range(2):
        zraw[r, SLOTS] = zero
        sraw[r, SLOTS] = zero
    zero16 = jnp.zeros((T, T), BF16)
    for a in range(8):
        for b in range(8):
            if abs(a - b) > 3:
                for ref in (zh, zl, zth, ztl):
                    ref[a * T : (a + 1) * T, b * T : (b + 1) * T] = zero16
    for base in (0, 2 * T):
        scat[base : base + T, 7 * T :] = zero16
        scat[base + T : base + 2 * T, :T] = zero16

    load_pat.wait()
    low = []
    for r in range(2):
        row = row_of(3 + r)
        low.append([None] + [
            (pat[s, row] == row_of(3 + r + OFFS[s - 1])).astype(jnp.int32) for s in range(1, SLOTS)
        ])

    def slot_of(r, p):
        here = jnp.int32(SLOTS) if p == 0 else p + low[r][p] * (SLOTS - p)
        return here if p == 5 else jnp.where(low[r][p + 1] == 1, p + 1, here)

    def present(w, column):
        p = OFFS.index(column - w) if column != w else None
        if p is None:
            return None
        row, want = row_of(w), row_of(column)
        found = jnp.int32(0)
        if p <= 4:
            found = found | (pat[p + 1, row] == want).astype(jnp.int32)
        if p >= 1:
            found = found | (pat[p, row] == want).astype(jnp.int32)
        return found.astype(F32)

    def masked(x, w, column):
        if abs(w - column) > 3:
            return jnp.zeros_like(x)
        m = present(w, column)
        return x if m is None else x * m

    slots = [[slot_of(r, p) for p in range(6)] for r in range(2)]

    def dense(ref, r, o):
        if o == 3:
            return ref[r, 0]
        return ref[r, slots[r][o if o < 3 else o - 1]]

    load_z.wait()
    for r in range(2):
        for o in range(7):
            zwin[3 + r, o] = dense(zraw, r, o)

    pl.semaphore_wait(barrier, 2)
    for by in (1, 2):
        pl.semaphore_signal(here.at[by - 1], inc=1, device_id=device(by), device_id_type=MESH)

    count = [0]
    started = []

    def copy(src, dst, by):
        k = count[0]
        count[0] += 1
        cp = pltpu.make_async_remote_copy(
            src_ref=src, dst_ref=dst, send_sem=ssem.at[k], recv_sem=rsem.at[k],
            device_id=device(by), device_id_type=MESH,
        )
        started.append(cp)
        return cp

    def send(src, dst, by):
        cp = copy(src, dst, by)
        cp.start()
        return cp

    def copy_z(row_from, row_to, o, n, by):
        return copy(zwin.at[row_from, pl.ds(o, n)], zwin.at[row_to, pl.ds(o, n)], by)

    def send_z(*where):
        cp = copy_z(*where)
        cp.start()
        return cp

    r1 = send_z(4, 2, 3, 4, 1)
    r2 = send_z(4, 2, 1, 2, 1)
    r3 = send_z(3, 1, 2, 3, 1)
    pl.semaphore_wait(here.at[0], 1)
    l1 = send_z(3, 5, 0, 4, -1)
    l2 = send_z(3, 5, 4, 2, -1)
    l3 = send_z(4, 6, 2, 3, -1)

    def place(w, offsets):
        for o in offsets:
            t = zwin[w, o]
            c = w + o - 3
            hi, lo = halves(t)
            here = (slice(w * T, (w + 1) * T), slice(c * T, (c + 1) * T))
            zh[here] = hi
            zl[here] = lo
            hi, lo = halves(t.T)
            there = here[::-1]
            zth[there] = hi
            ztl[there] = lo

    for r in range(2):
        place(3 + r, range(7))
    load_s.wait()
    for r in range(2):
        for o in range(7):
            hi, lo = halves(dense(sraw, r, o))
            c = r + o
            scat[r * T : (r + 1) * T, c * T : (c + 1) * T] = hi
            scat[(2 + r) * T : (3 + r) * T, c * T : (c + 1) * T] = lo

    f1, r4 = copy_z(2, 0, 3, 4, 1), copy_z(3, 1, 5, 2, 1)
    g1, l4 = copy_z(5, 7, 0, 4, -1), copy_z(4, 6, 0, 2, -1)

    def pass_on():
        r1.wait_recv()
        f1.start()
        r4.start()

    pl.when(jnp.logical_not(opens))(pass_on)
    l1.wait_recv()
    g1.start()
    l4.start()
    place(5, range(4))
    l2.wait_recv()
    place(5, range(4, 6))
    l3.wait_recv()
    place(6, range(2, 5))
    g1.wait_recv()
    place(7, range(4))

    def product(rows, columns):
        k, n = slice(rows[0] * T, rows[1] * T), slice(columns[0] * T, columns[1] * T)
        both = dot(scat[:, k], zh[k, n])
        return both[: 2 * T] + both[2 * T :] + dot(scat[: 2 * T, k], zl[k, n])

    def keep_product(x, first, ref, index):
        for n in range(x.shape[1] // T):
            for r in range(2):
                tile = x[r * T : (r + 1) * T, n * T : (n + 1) * T]
                ref[index(first + n, r)] = masked(tile, 3 + r, first + n)

    def by_column(c, r):
        return (c, r)

    keep_product(product((3, 8), (6, 8)), 6, psend, by_column)
    pr2 = send(psend.at[6], pcol.at[1, pl.ds(1, 2)], 1)
    pr0 = send(psend.at[7, pl.ds(1, 1)], pcol.at[0, pl.ds(0, 1)], 2)
    pl.when(opens)(pass_on)
    place(2, range(3, 7))
    keep_product(product((2, 8), (5, 6)), 5, psend, by_column)
    pr1 = send(psend.at[5], pcol.at[0, pl.ds(1, 2)], 1)
    r2.wait_recv()
    place(2, range(1, 3))
    r3.wait_recv()
    place(1, range(2, 5))
    f1.wait_recv()
    place(0, range(3, 7))
    keep_product(product((0, 6), (0, 3)), 0, psend, by_column)
    pl.semaphore_wait(here.at[1], 1)
    pl0 = send(psend.at[0, pl.ds(0, 1)], pcol.at[1, pl.ds(7, 1)], -2)
    pl2 = send(psend.at[2], pcol.at[1, pl.ds(5, 2)], -1)
    pl1 = send(psend.at[1], pcol.at[0, pl.ds(5, 2)], -1)
    r4.wait_recv()
    place(1, range(5, 7))
    l4.wait_recv()
    place(6, range(2))
    keep_product(product((0, 8), (3, 5)), 3, pcol, lambda c, r: (c - 3, 3 + r))

    identity = (
        lax.broadcasted_iota(jnp.int32, (T, T), 0) == lax.broadcasted_iota(jnp.int32, (T, T), 1)
    ).astype(F32)

    def banded(high, low_, cat, c):
        here = slice(c * T, (c + 7) * T)
        wide = dot(high[here, here], cat[c])
        return wide[:, :T] + wide[:, T:] + dot(low_[here, here], cat[c, :, :T])

    def gram(c):
        for n in range(7):
            hi, lo = halves(pcol[c, c + n])
            pcat[c, n * T : (n + 1) * T, :T] = hi
            pcat[c, n * T : (n + 1) * T, T:] = lo
        g = banded(zth, ztl, pcat, c)
        for n in range(7):
            w = c + n
            tile = -g[n * T : (n + 1) * T]
            if w == 3 + c:
                tile = tile + identity
            tile = masked(tile, w, 3 + c)
            dsend[c, w] = tile
            if w in (3, 4):
                drow[3 + c, w - 3] = tile
            hi, lo = halves(tile)
            dcat[c, n * T : (n + 1) * T, :T] = hi
            dcat[c, n * T : (n + 1) * T, T:] = lo

    def send_column(src, dst, c):
        if c == 0:
            far = send(src.at[0, pl.ds(0, 1)], dst.at[7, pl.ds(1, 1)], -2)
        else:
            far = send(src.at[1, pl.ds(7, 1)], dst.at[0, pl.ds(0, 1)], 2)
        return [
            far,
            send(src.at[c, pl.ds(5, 2)], dst.at[1 + c], 1),
            send(src.at[c, pl.ds(1, 2)], dst.at[5 + c], -1),
        ]

    def update(c):
        u = banded(zh, zl, dcat, c)
        for n in range(7):
            w = c + n
            tile = u[n * T : (n + 1) * T]
            usend[c, w] = tile
            if w in (3, 4):
                urow[3 + c, w - 3] = tile

    for cp in (pl0, pl2, pr2):
        cp.wait_recv()
    gram(1)
    dcps = send_column(dsend, drow, 1)
    for cp in (pr0, pr1, pl1):
        cp.wait_recv()
    gram(0)
    dcps += send_column(dsend, drow, 0)
    update(1)
    ucps = send_column(usend, urow, 1)
    update(0)
    ucps += send_column(usend, urow, 0)

    def column_of(r, s):
        if s == 0:
            return 3 + r
        position = s - low[r][s]
        return r + position + (position >= 3).astype(jnp.int32)

    for cp in dcps:
        cp.wait_recv()
    for r in range(2):
        for s in range(SLOTS):
            correction[r, s] = drow[column_of(r, s), r]
    for cp in ucps:
        cp.wait_recv()
    for r in range(2):
        for s in range(SLOTS):
            refined[r, s] = zraw[r, s] + 0.5 * urow[column_of(r, s), r]
    for cp in started:
        cp.wait_send()


COPIES = 10 + 6 + 12


def body(correlation, factor, pattern):
    hbm_space = pl.BlockSpec(memory_space=pltpu.HBM)
    out = pltpu.VMEM(factor.shape, F32)
    tiles = lambda *lead: pltpu.VMEM((*lead, T, T), F32)
    return pl.pallas_call(
        kernel,
        out_shape=(out, out),
        in_specs=[hbm_space] * 3,
        out_specs=(pl.BlockSpec(memory_space=pltpu.VMEM),) * 2,
        scratch_shapes=[
            pltpu.SMEM(pattern.T.shape, jnp.int32),
            tiles(2, SLOTS + 1),
            tiles(2, SLOTS + 1),
            tiles(8, 7),
            pltpu.VMEM((4 * T, 8 * T), BF16),
            *[pltpu.VMEM((8 * T, 8 * T), BF16)] * 4,
            tiles(8, 2),
            tiles(2, 8),
            pltpu.VMEM((2, 7 * T, 2 * T), BF16),
            tiles(2, 8),
            tiles(8, 2),
            pltpu.VMEM((2, 7 * T, 2 * T), BF16),
            tiles(2, 8),
            tiles(8, 2),
            pltpu.SemaphoreType.DMA((3,)),
            pltpu.SemaphoreType.DMA((COPIES,)),
            pltpu.SemaphoreType.DMA((COPIES,)),
            pltpu.SemaphoreType.REGULAR((2,)),
        ],
        compiler_params=pltpu.CompilerParams(
            collective_id=0, has_side_effects=True, vmem_limit_bytes=60 << 20
        ),
    )(correlation, factor, pattern.T)


def solution(mesh):
    rows = P(("blk", "sub"), None, None, None)
    return jax.shard_map(body, mesh=mesh, in_specs=(rows, rows, P()), out_specs=(rows, rows), check_vma=False)
```

```python
import jax
import jax.numpy as jnp
from jax import lax
from jax.experimental import pallas as pl
from jax.experimental.pallas import tpu as pltpu
from jax.sharding import PartitionSpec as P

T = 128
RING = 32
SLOTS = 6
OFFS = (-3, -2, -1, 1, 2, 3)
F32 = jnp.float32
BF16 = jnp.bfloat16
MESH = pl.DeviceIdType.MESH


def halves(x):
    hi = x.astype(BF16)
    return hi, (x - hi.astype(F32)).astype(BF16)


def dot(a, b):
    return jnp.dot(a, b, preferred_element_type=F32)


def kernel(
    corr_hbm, fact_hbm, pat_hbm, refined, correction,
    pat, zraw, sraw, zwin, scat, zh, zl, zth, ztl, psend, pcol, pcat,
    dsend, drow, dcat, usend, urow, lsem, ssem, rsem, here,
):
    blks, subs = lax.axis_size("blk"), lax.axis_size("sub")
    world = blks * subs
    rows_all = 2 * world
    blk, sub = lax.axis_index("blk"), lax.axis_index("sub")
    me = blk * subs + sub
    opens = (sub == 0) & (lax.rem(blk, RING) == 0)

    def device(by):
        d = lax.rem(me + by + world, world)
        return (lax.div(d, subs), lax.rem(d, subs))

    def row_of(w):
        return lax.rem(2 * me + (w - 3) + rows_all, rows_all)

    load_pat = pltpu.make_async_copy(pat_hbm, pat, lsem.at[0])
    load_z = pltpu.make_async_copy(fact_hbm, zraw.at[:, pl.ds(0, SLOTS)], lsem.at[1])
    load_s = pltpu.make_async_copy(corr_hbm, sraw.at[:, pl.ds(0, SLOTS)], lsem.at[2])
    load_z.start()
    load_pat.start()
    load_s.start()

    barrier = pltpu.get_barrier_semaphore()
    for partner in (device(-1), device(-2)):
        pl.semaphore_signal(barrier, inc=1, device_id=partner, device_id_type=MESH)

    zero = jnp.zeros((T, T), F32)
    for r in range(2):
        zraw[r, SLOTS] = zero
        sraw[r, SLOTS] = zero
    zero16 = jnp.zeros((T, T), BF16)
    for a in range(8):
        for b in range(8):
            if abs(a - b) > 3:
                for ref in (zh, zl, zth, ztl):
                    ref[a * T : (a + 1) * T, b * T : (b + 1) * T] = zero16
    for base in (0, 2 * T):
        scat[base : base + T, 7 * T :] = zero16
        scat[base + T : base + 2 * T, :T] = zero16

    load_pat.wait()
    low = []
    for r in range(2):
        row = row_of(3 + r)
        low.append([None] + [
            (pat[s, row] == row_of(3 + r + OFFS[s - 1])).astype(jnp.int32) for s in range(1, SLOTS)
        ])

    def slot_of(r, p):
        here = jnp.int32(SLOTS) if p == 0 else p + low[r][p] * (SLOTS - p)
        return here if p == 5 else jnp.where(low[r][p + 1] == 1, p + 1, here)

    def present(w, column):
        p = OFFS.index(column - w) if column != w else None
        if p is None:
            return None
        row, want = row_of(w), row_of(column)
        found = jnp.int32(0)
        if p <= 4:
            found = found | (pat[p + 1, row] == want).astype(jnp.int32)
        if p >= 1:
            found = found | (pat[p, row] == want).astype(jnp.int32)
        return found.astype(F32)

    def masked(x, w, column):
        if abs(w - column) > 3:
            return jnp.zeros_like(x)
        m = present(w, column)
        return x if m is None else x * m

    slots = [[slot_of(r, p) for p in range(6)] for r in range(2)]

    def dense(ref, r, o):
        if o == 3:
            return ref[r, 0]
        return ref[r, slots[r][o if o < 3 else o - 1]]

    load_z.wait()
    for r in range(2):
        for o in range(7):
            zwin[3 + r, o] = dense(zraw, r, o)

    pl.semaphore_wait(barrier, 2)
    for by in (1, 2):
        pl.semaphore_signal(here.at[by - 1], inc=1, device_id=device(by), device_id_type=MESH)

    count = [0]
    started = []

    def copy(src, dst, by):
        k = count[0]
        count[0] += 1
        cp = pltpu.make_async_remote_copy(
            src_ref=src, dst_ref=dst, send_sem=ssem.at[k], recv_sem=rsem.at[k],
            device_id=device(by), device_id_type=MESH,
        )
        started.append(cp)
        return cp

    def send(src, dst, by):
        cp = copy(src, dst, by)
        cp.start()
        return cp

    def copy_z(row_from, row_to, o, n, by):
        return copy(zwin.at[row_from, pl.ds(o, n)], zwin.at[row_to, pl.ds(o, n)], by)

    def send_z(*where):
        cp = copy_z(*where)
        cp.start()
        return cp

    r1 = send_z(4, 2, 3, 4, 1)
    r2 = send_z(4, 2, 1, 2, 1)
    r3 = send_z(3, 1, 2, 3, 1)
    pl.semaphore_wait(here.at[0], 1)
    l1 = send_z(3, 5, 0, 4, -1)
    l2 = send_z(3, 5, 4, 2, -1)
    l3 = send_z(4, 6, 2, 3, -1)

    def place(w, offsets):
        for o in offsets:
            t = zwin[w, o]
            c = w + o - 3
            hi, lo = halves(t)
            here = (slice(w * T, (w + 1) * T), slice(c * T, (c + 1) * T))
            zh[here] = hi
            zl[here] = lo
            hi, lo = halves(t.T)
            there = here[::-1]
            zth[there] = hi
            ztl[there] = lo

    for r in range(2):
        place(3 + r, range(7))
    load_s.wait()
    for r in range(2):
        for o in range(7):
            hi, lo = halves(dense(sraw, r, o))
            c = r + o
            scat[r * T : (r + 1) * T, c * T : (c + 1) * T] = hi
            scat[(2 + r) * T : (3 + r) * T, c * T : (c + 1) * T] = lo

    f1, r4 = copy_z(2, 0, 3, 4, 1), copy_z(3, 1, 5, 2, 1)
    g1, l4 = copy_z(5, 7, 0, 4, -1), copy_z(4, 6, 0, 2, -1)

    def pass_on():
        r1.wait_recv()
        f1.start()
        r4.start()

    pl.when(jnp.logical_not(opens))(pass_on)
    l1.wait_recv()
    g1.start()
    l4.start()
    place(5, range(4))
    l2.wait_recv()
    place(5, range(4, 6))
    l3.wait_recv()
    place(6, range(2, 5))
    g1.wait_recv()
    place(7, range(4))

    def product(rows, columns):
        k, n = slice(rows[0] * T, rows[1] * T), slice(columns[0] * T, columns[1] * T)
        both = dot(scat[:, k], zh[k, n])
        return both[: 2 * T] + both[2 * T :] + dot(scat[: 2 * T, k], zl[k, n])

    def keep_product(x, first, ref, index):
        for n in range(x.shape[1] // T):
            for r in range(2):
                tile = x[r * T : (r + 1) * T, n * T : (n + 1) * T]
                ref[index(first + n, r)] = masked(tile, 3 + r, first + n)

    def by_column(c, r):
        return (c, r)

    keep_product(product((3, 8), (6, 8)), 6, psend, by_column)
    pr2 = send(psend.at[6], pcol.at[1, pl.ds(1, 2)], 1)
    pr0 = send(psend.at[7, pl.ds(1, 1)], pcol.at[0, pl.ds(0, 1)], 2)
    pl.when(opens)(pass_on)
    place(2, range(3, 7))
    keep_product(product((2, 8), (5, 6)), 5, psend, by_column)
    pr1 = send(psend.at[5], pcol.at[0, pl.ds(1, 2)], 1)
    r2.wait_recv()
    place(2, range(1, 3))
    r3.wait_recv()
    place(1, range(2, 5))
    f1.wait_recv()
    place(0, range(3, 7))
    keep_product(product((0, 6), (0, 3)), 0, psend, by_column)
    pl.semaphore_wait(here.at[1], 1)
    pl0 = send(psend.at[0, pl.ds(0, 1)], pcol.at[1, pl.ds(7, 1)], -2)
    pl2 = send(psend.at[2], pcol.at[1, pl.ds(5, 2)], -1)
    pl1 = send(psend.at[1], pcol.at[0, pl.ds(5, 2)], -1)
    r4.wait_recv()
    place(1, range(5, 7))
    l4.wait_recv()
    place(6, range(2))
    keep_product(product((0, 8), (3, 5)), 3, pcol, lambda c, r: (c - 3, 3 + r))

    identity = (
        lax.broadcasted_iota(jnp.int32, (T, T), 0) == lax.broadcasted_iota(jnp.int32, (T, T), 1)
    ).astype(F32)

    def banded(high, low_, cat, c):
        here = slice(c * T, (c + 7) * T)
        wide = dot(high[here, here], cat[c])
        return wide[:, :T] + wide[:, T:] + dot(low_[here, here], cat[c, :, :T])

    def gram(c):
        for n in range(7):
            hi, lo = halves(pcol[c, c + n])
            pcat[c, n * T : (n + 1) * T, :T] = hi
            pcat[c, n * T : (n + 1) * T, T:] = lo
        g = banded(zth, ztl, pcat, c)
        for n in range(7):
            w = c + n
            tile = -g[n * T : (n + 1) * T]
            if w == 3 + c:
                tile = tile + identity
            tile = masked(tile, w, 3 + c)
            dsend[c, w] = tile
            if w in (3, 4):
                drow[3 + c, w - 3] = tile
            hi, lo = halves(tile)
            dcat[c, n * T : (n + 1) * T, :T] = hi
            dcat[c, n * T : (n + 1) * T, T:] = lo

    def send_column(src, dst, c):
        if c == 0:
            far = send(src.at[0, pl.ds(0, 1)], dst.at[7, pl.ds(1, 1)], -2)
        else:
            far = send(src.at[1, pl.ds(7, 1)], dst.at[0, pl.ds(0, 1)], 2)
        return [
            far,
            send(src.at[c, pl.ds(5, 2)], dst.at[1 + c], 1),
            send(src.at[c, pl.ds(1, 2)], dst.at[5 + c], -1),
        ]

    def update(c):
        u = banded(zh, zl, dcat, c)
        for n in range(7):
            w = c + n
            tile = u[n * T : (n + 1) * T]
            usend[c, w] = tile
            if w in (3, 4):
                urow[3 + c, w - 3] = tile

    for cp in (pl0, pl2, pr2):
        cp.wait_recv()
    gram(1)
    dcps = send_column(dsend, drow, 1)
    for cp in (pr0, pr1, pl1):
        cp.wait_recv()
    gram(0)
    dcps += send_column(dsend, drow, 0)
    update(1)
    ucps = send_column(usend, urow, 1)
    update(0)
    ucps += send_column(usend, urow, 0)

    def column_of(r, s):
        if s == 0:
            return 3 + r
        position = s - low[r][s]
        return r + position + (position >= 3).astype(jnp.int32)

    for cp in dcps:
        cp.wait_recv()
    for r in range(2):
        for s in range(SLOTS):
            correction[r, s] = drow[column_of(r, s), r]
    for cp in ucps:
        cp.wait_recv()
    for r in range(2):
        for s in range(SLOTS):
            refined[r, s] = zraw[r, s] + 0.5 * urow[column_of(r, s), r]
    for cp in started:
        cp.wait_send()


def store(refined, correction, refined_hbm, correction_hbm, sem):
    copies = [
        pltpu.make_async_copy(src.at[r], dst.at[r], sem.at[2 * n + r])
        for n, (src, dst) in enumerate(((refined, refined_hbm), (correction, correction_hbm)))
        for r in range(2)
    ]
    for cp in copies:
        cp.start()
    for cp in copies:
        cp.wait()


COPIES = 10 + 6 + 12


def body(correlation, factor, pattern):
    hbm_space = pl.BlockSpec(memory_space=pltpu.HBM)
    out = pltpu.VMEM(factor.shape, F32)
    tiles = lambda *lead: pltpu.VMEM((*lead, T, T), F32)
    done = pl.pallas_call(
        kernel,
        out_shape=(out, out),
        in_specs=[hbm_space] * 3,
        out_specs=(pl.BlockSpec(memory_space=pltpu.VMEM),) * 2,
        scratch_shapes=[
            pltpu.SMEM(pattern.T.shape, jnp.int32),
            tiles(2, SLOTS + 1),
            tiles(2, SLOTS + 1),
            tiles(8, 7),
            pltpu.VMEM((4 * T, 8 * T), BF16),
            *[pltpu.VMEM((8 * T, 8 * T), BF16)] * 4,
            tiles(8, 2),
            tiles(2, 8),
            pltpu.VMEM((2, 7 * T, 2 * T), BF16),
            tiles(2, 8),
            tiles(8, 2),
            pltpu.VMEM((2, 7 * T, 2 * T), BF16),
            tiles(2, 8),
            tiles(8, 2),
            pltpu.SemaphoreType.DMA((3,)),
            pltpu.SemaphoreType.DMA((COPIES,)),
            pltpu.SemaphoreType.DMA((COPIES,)),
            pltpu.SemaphoreType.REGULAR((2,)),
        ],
        compiler_params=pltpu.CompilerParams(
            collective_id=0, has_side_effects=True, vmem_limit_bytes=60 << 20
        ),
    )(correlation, factor, pattern.T)
    return pl.pallas_call(
        store,
        out_shape=(pltpu.HBM(factor.shape, F32),) * 2,
        in_specs=[pl.BlockSpec(memory_space=pl.ANY)] * 2,
        out_specs=(pl.BlockSpec(memory_space=pltpu.HBM),) * 2,
        scratch_shapes=[pltpu.SemaphoreType.DMA((4,))],
        compiler_params=pltpu.CompilerParams(vmem_limit_bytes=4 << 20),
    )(*done)


def solution(mesh):
    rows = P(("blk", "sub"), None, None, None)
    return jax.shard_map(body, mesh=mesh, in_specs=(rows, rows, P()), out_specs=(rows, rows), check_vma=False)
```

```python
import jax
import jax.numpy as jnp
from jax import lax
from jax.experimental import pallas as pl
from jax.experimental.pallas import tpu as pltpu
from jax.sharding import PartitionSpec as P

T = 128
RING = 32
SLOTS = 6
OFFS = (-3, -2, -1, 1, 2, 3)
F32 = jnp.float32
BF16 = jnp.bfloat16
MESH = pl.DeviceIdType.MESH


def halves(x):
    hi = x.astype(BF16)
    return hi, (x - hi.astype(F32)).astype(BF16)


def dot(a, b):
    return jnp.dot(a, b, preferred_element_type=F32)


def kernel(
    corr_hbm, fact_hbm, pat_hbm, refined, correction,
    pat, zraw, sraw, zwin, scat, zh, zl, zth, ztl, psend, pcol, pcat,
    dsend, drow, dcat, usend, urow, lsem, ssem, rsem, here,
):
    blks, subs = lax.axis_size("blk"), lax.axis_size("sub")
    world = blks * subs
    rows_all = 2 * world
    blk, sub = lax.axis_index("blk"), lax.axis_index("sub")
    me = blk * subs + sub
    opens = (sub == 0) & (lax.rem(blk, RING) == 0)

    def device(by):
        d = lax.rem(me + by + world, world)
        return (lax.div(d, subs), lax.rem(d, subs))

    def row_of(w):
        return lax.rem(2 * me + (w - 3) + rows_all, rows_all)

    load_pat = pltpu.make_async_copy(pat_hbm, pat, lsem.at[0])
    load_z = pltpu.make_async_copy(fact_hbm, zraw.at[:, pl.ds(0, SLOTS)], lsem.at[1])
    load_s = pltpu.make_async_copy(corr_hbm, sraw.at[:, pl.ds(0, SLOTS)], lsem.at[2])
    load_z.start()
    load_pat.start()
    load_s.start()

    barrier = pltpu.get_barrier_semaphore()
    for partner in (device(-1), device(-2)):
        pl.semaphore_signal(barrier, inc=1, device_id=partner, device_id_type=MESH)

    zero = jnp.zeros((T, T), F32)
    for r in range(2):
        zraw[r, SLOTS] = zero
        sraw[r, SLOTS] = zero
    zero16 = jnp.zeros((T, T), BF16)
    for a in range(8):
        for b in range(8):
            if abs(a - b) > 3:
                for ref in (zh, zl, zth, ztl):
                    ref[a * T : (a + 1) * T, b * T : (b + 1) * T] = zero16
    for base in (0, 2 * T):
        scat[base : base + T, 7 * T :] = zero16
        scat[base + T : base + 2 * T, :T] = zero16

    load_pat.wait()
    low = []
    for r in range(2):
        row = row_of(3 + r)
        low.append([None] + [
            (pat[s, row] == row_of(3 + r + OFFS[s - 1])).astype(jnp.int32) for s in range(1, SLOTS)
        ])

    def slot_of(r, p):
        here = jnp.int32(SLOTS) if p == 0 else p + low[r][p] * (SLOTS - p)
        return here if p == 5 else jnp.where(low[r][p + 1] == 1, p + 1, here)

    def present(w, column):
        p = OFFS.index(column - w) if column != w else None
        if p is None:
            return None
        row, want = row_of(w), row_of(column)
        found = jnp.int32(0)
        if p <= 4:
            found = found | (pat[p + 1, row] == want).astype(jnp.int32)
        if p >= 1:
            found = found | (pat[p, row] == want).astype(jnp.int32)
        return found.astype(F32)

    def masked(x, w, column):
        if abs(w - column) > 3:
            return jnp.zeros_like(x)
        m = present(w, column)
        return x if m is None else x * m

    slots = [[slot_of(r, p) for p in range(6)] for r in range(2)]

    def dense(ref, r, o):
        if o == 3:
            return ref[r, 0]
        return ref[r, slots[r][o if o < 3 else o - 1]]

    load_z.wait()
    for r in range(2):
        for o in range(7):
            zwin[3 + r, o] = dense(zraw, r, o)

    pl.semaphore_wait(barrier, 2)
    for by in (1, 2):
        pl.semaphore_signal(here.at[by - 1], inc=1, device_id=device(by), device_id_type=MESH)

    count = [0]
    started = []

    def copy(src, dst, by):
        k = count[0]
        count[0] += 1
        cp = pltpu.make_async_remote_copy(
            src_ref=src, dst_ref=dst, send_sem=ssem.at[k], recv_sem=rsem.at[k],
            device_id=device(by), device_id_type=MESH,
        )
        started.append(cp)
        return cp

    def send(src, dst, by):
        cp = copy(src, dst, by)
        cp.start()
        return cp

    def copy_z(row_from, row_to, o, n, by):
        return copy(zwin.at[row_from, pl.ds(o, n)], zwin.at[row_to, pl.ds(o, n)], by)

    def send_z(*where):
        cp = copy_z(*where)
        cp.start()
        return cp

    r1 = send_z(4, 2, 3, 4, 1)
    r2 = send_z(4, 2, 1, 2, 1)
    r3 = send_z(3, 1, 2, 3, 1)
    pl.semaphore_wait(here.at[0], 1)
    l1 = send_z(3, 5, 0, 4, -1)
    l2 = send_z(3, 5, 4, 2, -1)
    l3 = send_z(4, 6, 2, 3, -1)

    def place(w, offsets):
        for o in offsets:
            t = zwin[w, o]
            c = w + o - 3
            hi, lo = halves(t)
            here = (slice(w * T, (w + 1) * T), slice(c * T, (c + 1) * T))
            zh[here] = hi
            zl[here] = lo
            hi, lo = halves(t.T)
            there = here[::-1]
            zth[there] = hi
            ztl[there] = lo

    for r in range(2):
        place(3 + r, range(7))
    load_s.wait()
    for r in range(2):
        for o in range(7):
            hi, lo = halves(dense(sraw, r, o))
            c = r + o
            scat[r * T : (r + 1) * T, c * T : (c + 1) * T] = hi
            scat[(2 + r) * T : (3 + r) * T, c * T : (c + 1) * T] = lo

    f1, r4 = copy_z(2, 0, 3, 4, 1), copy_z(3, 1, 5, 2, 1)
    g1, l4 = copy_z(5, 7, 0, 4, -1), copy_z(4, 6, 0, 2, -1)

    def pass_on():
        r1.wait_recv()
        f1.start()

    pl.when(jnp.logical_not(opens))(pass_on)
    r4.start()
    l1.wait_recv()
    g1.start()
    l4.start()
    place(5, range(4))
    l2.wait_recv()
    place(5, range(4, 6))
    l3.wait_recv()
    place(6, range(2, 5))
    g1.wait_recv()
    place(7, range(4))

    def product(rows, columns):
        k, n = slice(rows[0] * T, rows[1] * T), slice(columns[0] * T, columns[1] * T)
        both = dot(scat[:, k], zh[k, n])
        return both[: 2 * T] + both[2 * T :] + dot(scat[: 2 * T, k], zl[k, n])

    def keep_product(x, first, ref, index):
        for n in range(x.shape[1] // T):
            for r in range(2):
                tile = x[r * T : (r + 1) * T, n * T : (n + 1) * T]
                ref[index(first + n, r)] = masked(tile, 3 + r, first + n)

    def by_column(c, r):
        return (c, r)

    keep_product(product((3, 8), (6, 8)), 6, psend, by_column)
    pr2 = send(psend.at[6], pcol.at[1, pl.ds(1, 2)], 1)
    pr0 = send(psend.at[7, pl.ds(1, 1)], pcol.at[0, pl.ds(0, 1)], 2)
    pl.when(opens)(pass_on)
    place(2, range(3, 7))
    keep_product(product((2, 8), (5, 6)), 5, psend, by_column)
    pr1 = send(psend.at[5], pcol.at[0, pl.ds(1, 2)], 1)
    r2.wait_recv()
    place(2, range(1, 3))
    r3.wait_recv()
    place(1, range(2, 5))
    f1.wait_recv()
    place(0, range(3, 7))
    keep_product(product((0, 6), (0, 3)), 0, psend, by_column)
    pl.semaphore_wait(here.at[1], 1)
    pl0 = send(psend.at[0, pl.ds(0, 1)], pcol.at[1, pl.ds(7, 1)], -2)
    pl2 = send(psend.at[2], pcol.at[1, pl.ds(5, 2)], -1)
    pl1 = send(psend.at[1], pcol.at[0, pl.ds(5, 2)], -1)
    r4.wait_recv()
    place(1, range(5, 7))
    l4.wait_recv()
    place(6, range(2))
    keep_product(product((0, 8), (3, 5)), 3, pcol, lambda c, r: (c - 3, 3 + r))

    identity = (
        lax.broadcasted_iota(jnp.int32, (T, T), 0) == lax.broadcasted_iota(jnp.int32, (T, T), 1)
    ).astype(F32)

    def banded(high, low_, cat, c):
        here = slice(c * T, (c + 7) * T)
        wide = dot(high[here, here], cat[c])
        return wide[:, :T] + wide[:, T:] + dot(low_[here, here], cat[c, :, :T])

    def gram(c):
        for n in range(7):
            hi, lo = halves(pcol[c, c + n])
            pcat[c, n * T : (n + 1) * T, :T] = hi
            pcat[c, n * T : (n + 1) * T, T:] = lo
        g = banded(zth, ztl, pcat, c)
        for n in range(7):
            w = c + n
            tile = -g[n * T : (n + 1) * T]
            if w == 3 + c:
                tile = tile + identity
            tile = masked(tile, w, 3 + c)
            dsend[c, w] = tile
            if w in (3, 4):
                drow[3 + c, w - 3] = tile
            hi, lo = halves(tile)
            dcat[c, n * T : (n + 1) * T, :T] = hi
            dcat[c, n * T : (n + 1) * T, T:] = lo

    def send_column(src, dst, c):
        if c == 0:
            far = send(src.at[0, pl.ds(0, 1)], dst.at[7, pl.ds(1, 1)], -2)
        else:
            far = send(src.at[1, pl.ds(7, 1)], dst.at[0, pl.ds(0, 1)], 2)
        return [
            far,
            send(src.at[c, pl.ds(5, 2)], dst.at[1 + c], 1),
            send(src.at[c, pl.ds(1, 2)], dst.at[5 + c], -1),
        ]

    def update(c):
        u = banded(zh, zl, dcat, c)
        for n in range(7):
            w = c + n
            tile = u[n * T : (n + 1) * T]
            usend[c, w] = tile
            if w in (3, 4):
                urow[3 + c, w - 3] = tile

    for cp in (pl0, pl2, pr2):
        cp.wait_recv()
    gram(1)
    dcps = send_column(dsend, drow, 1)
    for cp in (pr0, pr1, pl1):
        cp.wait_recv()
    gram(0)
    dcps += send_column(dsend, drow, 0)
    update(1)
    ucps = send_column(usend, urow, 1)
    update(0)
    ucps += send_column(usend, urow, 0)

    def column_of(r, s):
        if s == 0:
            return 3 + r
        position = s - low[r][s]
        return r + position + (position >= 3).astype(jnp.int32)

    for cp in dcps:
        cp.wait_recv()
    for r in range(2):
        for s in range(SLOTS):
            correction[r, s] = drow[column_of(r, s), r]
    for cp in ucps:
        cp.wait_recv()
    for r in range(2):
        for s in range(SLOTS):
            refined[r, s] = zraw[r, s] + 0.5 * urow[column_of(r, s), r]
    for cp in started:
        cp.wait_send()


def store(refined, correction, refined_hbm, correction_hbm, sem):
    copies = [
        pltpu.make_async_copy(src.at[r], dst.at[r], sem.at[2 * n + r])
        for n, (src, dst) in enumerate(((refined, refined_hbm), (correction, correction_hbm)))
        for r in range(2)
    ]
    for cp in copies:
        cp.start()
    for cp in copies:
        cp.wait()


COPIES = 10 + 6 + 12


def body(correlation, factor, pattern):
    hbm_space = pl.BlockSpec(memory_space=pltpu.HBM)
    out = pltpu.VMEM(factor.shape, F32)
    tiles = lambda *lead: pltpu.VMEM((*lead, T, T), F32)
    done = pl.pallas_call(
        kernel,
        out_shape=(out, out),
        in_specs=[hbm_space] * 3,
        out_specs=(pl.BlockSpec(memory_space=pltpu.VMEM),) * 2,
        scratch_shapes=[
            pltpu.SMEM(pattern.T.shape, jnp.int32),
            tiles(2, SLOTS + 1),
            tiles(2, SLOTS + 1),
            tiles(8, 7),
            pltpu.VMEM((4 * T, 8 * T), BF16),
            *[pltpu.VMEM((8 * T, 8 * T), BF16)] * 4,
            tiles(8, 2),
            tiles(2, 8),
            pltpu.VMEM((2, 7 * T, 2 * T), BF16),
            tiles(2, 8),
            tiles(8, 2),
            pltpu.VMEM((2, 7 * T, 2 * T), BF16),
            tiles(2, 8),
            tiles(8, 2),
            pltpu.SemaphoreType.DMA((3,)),
            pltpu.SemaphoreType.DMA((COPIES,)),
            pltpu.SemaphoreType.DMA((COPIES,)),
            pltpu.SemaphoreType.REGULAR((2,)),
        ],
        compiler_params=pltpu.CompilerParams(
            collective_id=0, has_side_effects=True, vmem_limit_bytes=60 << 20
        ),
    )(correlation, factor, pattern.T)
    return pl.pallas_call(
        store,
        out_shape=(pltpu.HBM(factor.shape, F32),) * 2,
        in_specs=[pl.BlockSpec(memory_space=pl.ANY)] * 2,
        out_specs=(pl.BlockSpec(memory_space=pltpu.HBM),) * 2,
        scratch_shapes=[pltpu.SemaphoreType.DMA((4,))],
        compiler_params=pltpu.CompilerParams(vmem_limit_bytes=4 << 20),
    )(*done)


def solution(mesh):
    rows = P(("blk", "sub"), None, None, None)
    return jax.shard_map(body, mesh=mesh, in_specs=(rows, rows, P()), out_specs=(rows, rows), check_vma=False)
```
